32 devices in a mesh: dp: 8 (over y, x, core), tensor: 4 (over z).
Axes of the slice: x: 2, y: 2, z: 4, core: 2. Of those that a mesh axis runs over, the one named last changes fastest.
Arguments:
- tokens: bfloat16 [16384, 1024], P(('dp', 'tensor')), may hold values from -16 to 16
- prompts: bfloat16 [8, 64, 1024], P('dp'), may hold values from -6 to 6
- w_attn: bfloat16 [3, 1024, 1024], P(None, None, 'tensor'), may hold values from -0.1875 to 0.1875
- w_out: bfloat16 [1024, 1024], P('tensor'), may hold values from -0.1875 to 0.1875
- norm_gain: float32 [2, 1024], replicated, may hold values from 0.1 to 1.9
- norm_bias: float32 [2, 1024], replicated, may hold values from -3 to 3
- w_in: bfloat16 [1024, 4096], P(None, 'tensor'), may hold values from -0.1875 to 0.1875
- b_in: float32 [4096], P('tensor'), may hold values from -3 to 3
- w_down: bfloat16 [4096, 1024], P('tensor'), may hold values from -0.09375 to 0.09375
- index_rows: bfloat16 [16384, 1024], P('dp'), may hold values from -6 to 6
- lengths: int32 [8, 32], P('dp'), may hold values from 1 to 512, 2048 in all within a row
- groups: int32 [256], P('dp'), may hold values from 0 to 7
- candidates: int32 [256, 64], P(('dp', 'tensor')), may hold values from 0 to 16383
Outputs:
- scores: float32 [256, 64], P(('dp', 'tensor'))
The draws below stay inside these ranges and needn't reach their ends.
All inputs are finite; a program needn't handle non-finite values.
Results may differ from the reference program's by a relative error of at most 0.01.
Values may be sent and summed in bfloat16 or wider, within the bound.
A program may use at most 128 MiB of HBM per device.

```python
import math
import jax
import jax.numpy as jnp
import numpy as np
from jax import lax

D = 1024
HEADS = 16
FF = 4096
HEAD_DIM = 64
TOK_DEV = 2048
TEXTS_DEV = 32
MAXLEN = 512
PLEN = 64
CANDS = 64
TOKENS = 16384
TEXTS = 256
GROUPS = 8
INDEX = 16384
N_DP = 8


def draw_tokens(key, part):
    first = jax.random.fold_in(jax.random.fold_in(key, 11), 0)
    base = jnp.clip(jax.random.normal(first, (TOKENS, D), jnp.float32), -6.0, 6.0)
    return base.astype(jnp.bfloat16)


def plant(entries, stream_key, least, high):
    place = [jax.random.randint(jax.random.fold_in(stream_key, axis), (), 0, length) for axis, length in enumerate(entries.shape)]
    main_axis = entries.shape.index(max(entries.shape))
    beside = place[:main_axis] + [(place[main_axis] + 1) % entries.shape[main_axis]] + place[main_axis + 1:]
    return entries.at[tuple(place)].set(least).at[tuple(beside)].set(high)


def block_levels(rng, extent, pieces, low, top_value):
    def one(dim, blocks):
        heights = jax.random.uniform(jax.random.fold_in(jax.random.fold_in(rng, 6), dim), (blocks,), jnp.float32, low / len(pieces), top_value / len(pieces))
        return jnp.repeat(jnp.exp(heights), extent[dim] // blocks).reshape((-1,) + (1,) * (len(extent) - dim - 1))

    loudness = one(*pieces[0])
    for cut in pieces[1:]:
        loudness = loudness * one(*cut)
    return loudness


def rank_table(amount, slope):
    loads = [(1 << 20) // math.isqrt(standing ** slope) + 1 for standing in range(1, amount + 1)]
    deviation = 1 + sum(loads) // (1 << 30)
    return np.cumsum(np.array([max(1, weight // deviation) for weight in loads]))


def ranked(own_key, shape, number_of, lean):
    table = rank_table(number_of, lean)
    lot = jax.random.randint(jax.random.fold_in(own_key, 1), shape, 0, int(table[number_of - 1]))
    rank = jnp.searchsorted(jnp.asarray(table, jnp.int32), lot, side="right")
    return jax.random.permutation(jax.random.fold_in(own_key, 2), number_of)[rank].astype(jnp.int32)


def length_profile(amount, total, most, slope):
    weights = [(1 << 20) // math.isqrt(grade ** slope) + 1 for grade in range(2, amount + 1)]
    spare, given = total - most - (amount - 1), [1] * (amount - 1)
    while spare > 0:
        free = [i for i in range(amount - 1) if given[i] < most]
        mass, budget = sum([weights[i] for i in free]), spare
        for i in free:
            extra = min(most - given[i], max(1, budget * weights[i] // mass), spare)
            given[i] = given[i] + extra
            spare = spare - extra
    return np.array([most] + given)


def uneven(key, number_of, total, limit, slope):
    if number_of == 2:
        one = jax.random.randint(key, (), max(1, total - limit), min(limit, total - 1) + 1)
        return jnp.stack([one, total - one])
    sizes = jnp.asarray(length_profile(number_of, total, limit, slope), jnp.int32)
    pairs = (number_of - 1) // 2
    source_of, sink = sizes[1:1 + 2 * pairs:2], sizes[2:2 + 2 * pairs:2]
    room = jnp.minimum(source_of - 1, limit - sink)
    passed = jax.random.randint(jax.random.fold_in(key, 1), (pairs,), 0, 1 << 20) % (room + 1)
    sizes = sizes.at[1:1 + 2 * pairs:2].set(source_of - passed).at[2:2 + 2 * pairs:2].set(sink + passed)
    return sizes[jax.random.permutation(jax.random.fold_in(key, 2), number_of)]


def bell_draw(stream_key, extent, spread, most, shards=(), held_as=jnp.bfloat16):
    loudness = block_levels(stream_key, extent, shards, -0.22, 0.18) if shards else 1.0
    values = jax.random.normal(stream_key, extent, jnp.float32) * spread * loudness
    return jnp.minimum(jnp.maximum(values, -most), most).astype(held_as)


def setup_inputs(seed: int = 0) -> dict:
    arg_keys = jax.random.split(jax.random.key(seed), 14)
    return {
        "tokens": draw_tokens(jax.random.fold_in(arg_keys[13], 71), 0),
        "prompts": bell_draw(arg_keys[1], (GROUPS, PLEN, D), 1.0, 6.0, ((0, 8),)),
        "w_attn": bell_draw(arg_keys[2], (3, D, D), D ** -0.5, 0.1875, ((2, 4),)),
        "w_out": bell_draw(arg_keys[3], (D, D), D ** -0.5, 0.1875, ((0, 4),)),
        "norm_gain": jnp.clip(1.0 + 0.18 * jax.random.normal(arg_keys[4], (2, D), jnp.float32), 0.1, 1.9),
        "norm_bias": bell_draw(arg_keys[5], (2, D), 0.5, 3.0, (), jnp.float32),
        "w_in": bell_draw(arg_keys[6], (D, FF), D ** -0.5, 0.1875, ((1, 4),)),
        "b_in": bell_draw(arg_keys[7], (FF,), 0.5, 3.0, ((0, 4),), jnp.float32),
        "w_down": bell_draw(arg_keys[8], (FF, D), FF ** -0.5, 0.09375, ((0, 4),)),
        "index_rows": bell_draw(arg_keys[9], (INDEX, D), 1.0, 6.0, ((0, 8),)),
        "lengths": jax.vmap(lambda own: uneven(own, TEXTS_DEV, TOK_DEV, MAXLEN, 2))(jax.random.split(arg_keys[10], N_DP)).reshape((N_DP, TEXTS_DEV)).astype(jnp.int32),
        "groups": plant(ranked(arg_keys[11], (TEXTS,), GROUPS, 1), jax.random.fold_in(arg_keys[11], 3), 0, GROUPS - 1).astype(jnp.int32),
        "candidates": plant(jax.random.randint(arg_keys[12], (TEXTS, CANDS), 0, INDEX), jax.random.fold_in(arg_keys[12], 1), 0, INDEX - 1).astype(jnp.int32),
    }


def layer_norm(values, gain, bias):
    mean = lax.optimization_barrier(jnp.mean(values, axis=-1, keepdims=True))
    centred = values - mean
    var = lax.optimization_barrier(jnp.mean(centred * centred, axis=-1, keepdims=True))
    return centred * lax.rsqrt(var + 1e-05) * gain + bias

def reference(tokens, prompts, w_attn, w_out, norm_gain, norm_bias, w_in, b_in, w_down, index_rows, lengths, groups, candidates):
    scale = HEAD_DIM ** (-0.5)
    flat_prompts = prompts.reshape(GROUPS * PLEN, D)
    prompt_key = jnp.dot(flat_prompts, w_attn[1], preferred_element_type=jnp.float32).astype(jnp.bfloat16)
    prompt_value = jnp.dot(flat_prompts, w_attn[2], preferred_element_type=jnp.float32).astype(jnp.bfloat16)
    key_group = jnp.arange(GROUPS * PLEN, dtype=jnp.int32) // PLEN
    text_ids = jnp.arange(TEXTS_DEV, dtype=jnp.int32)

    def one_pack(packed):
        block, lens, grp = packed
        ends = jnp.cumsum(lens).astype(jnp.int32)
        position = jnp.arange(TOK_DEV, dtype=jnp.int32)
        seg = lax.optimization_barrier(jnp.sum((position[:, None] >= ends[None, :]).astype(jnp.int32), axis=1)).astype(jnp.int32)
        same_text = seg[:, None] == text_ids[None, :]
        tok_group = lax.optimization_barrier(jnp.sum(jnp.where(same_text, grp[None, :], 0), axis=1)).astype(jnp.int32)
        query = (jnp.dot(block, w_attn[0], preferred_element_type=jnp.float32) * scale).astype(jnp.bfloat16)
        keys = jnp.dot(block, w_attn[1], preferred_element_type=jnp.float32).astype(jnp.bfloat16)
        values = jnp.dot(block, w_attn[2], preferred_element_type=jnp.float32).astype(jnp.bfloat16)
        allowed = jnp.concatenate([seg[:, None] == seg[None, :], tok_group[:, None] == key_group[None, :]], axis=1)

        def one_head(head):
            start = head * HEAD_DIM
            q_head = lax.dynamic_slice_in_dim(query, start, HEAD_DIM, 1)
            k_head = jnp.concatenate([lax.dynamic_slice_in_dim(keys, start, HEAD_DIM, 1), lax.dynamic_slice_in_dim(prompt_key, start, HEAD_DIM, 1)], axis=0)
            v_head = jnp.concatenate([lax.dynamic_slice_in_dim(values, start, HEAD_DIM, 1), lax.dynamic_slice_in_dim(prompt_value, start, HEAD_DIM, 1)], axis=0)
            logits = jnp.dot(q_head, k_head.T, preferred_element_type=jnp.float32)
            logits = jnp.where(allowed, logits, jnp.float32(-1e+30))
            top = lax.optimization_barrier(jnp.max(logits, axis=1, keepdims=True))
            weights = jnp.exp(logits - top)
            total = lax.optimization_barrier(jnp.sum(weights, axis=1, keepdims=True))
            probs = (weights / total).astype(jnp.bfloat16)
            return jnp.dot(probs, v_head, preferred_element_type=jnp.float32).astype(jnp.bfloat16)
        context = lax.map(one_head, jnp.arange(HEADS, dtype=jnp.int32))
        context = jnp.transpose(context, (1, 0, 2)).reshape(TOK_DEV, D)
        attended = jnp.dot(context, w_out, preferred_element_type=jnp.float32)
        normed = layer_norm(block.astype(jnp.float32) + attended, norm_gain[0], norm_bias[0]).astype(jnp.bfloat16)
        expanded = jax.nn.gelu(jnp.dot(normed, w_in, preferred_element_type=jnp.float32) + b_in, approximate=False).astype(jnp.bfloat16)
        reduced = jnp.dot(expanded, w_down, preferred_element_type=jnp.float32)
        output = layer_norm(normed.astype(jnp.float32) + reduced, norm_gain[1], norm_bias[1]).astype(jnp.bfloat16)
        member = (text_ids[:, None] == seg[None, :]).astype(jnp.bfloat16)
        sums = jnp.dot(member, output, preferred_element_type=jnp.float32)
        pooled = sums / lens[:, None].astype(jnp.float32)
        square = lax.optimization_barrier(jnp.mean(pooled * pooled, axis=1, keepdims=True))
        return (pooled * lax.rsqrt(square + 1e-06)).astype(jnp.bfloat16)
    embedded = lax.map(one_pack, (tokens.reshape(N_DP, TOK_DEV, D), lengths, groups.reshape(N_DP, TEXTS_DEV)))
    embedded = embedded.reshape(TEXTS, D)

    def one_text(pair):
        vector, chosen = pair
        rows = jnp.take(index_rows, chosen, axis=0)
        return jnp.dot(rows, vector, preferred_element_type=jnp.float32) * D ** (-0.5)
    return lax.map(one_text, (embedded, candidates))
```

```python
import jax
import jax.numpy as jnp
from jax import lax
from jax.sharding import PartitionSpec as P

D = 1024
HEAD_DIM = 64


def layer_norm(values, gain, bias):
    mean = jnp.mean(values, axis=-1, keepdims=True)
    centred = values - mean
    var = jnp.mean(centred * centred, axis=-1, keepdims=True)
    return centred * lax.rsqrt(var + 1e-05) * gain + bias


def project(block, weight):
    return jnp.dot(block, weight, preferred_element_type=jnp.float32).astype(jnp.bfloat16)


def shards(
    tokens,
    prompts,
    w_attn,
    w_out,
    norm_gain,
    norm_bias,
    w_in,
    b_in,
    w_down,
    index_rows,
    lengths,
    groups,
    candidates,
):
    shard_rows = tokens.shape[0]
    tok_dev = shard_rows * lax.axis_size("tensor")
    columns = w_attn.shape[2]
    heads_here = columns // HEAD_DIM
    scale = HEAD_DIM ** (-0.5)
    whole = lax.all_gather(tokens, "tensor", axis=0, tiled=True)
    query = (jnp.dot(whole, w_attn[0], preferred_element_type=jnp.float32) * scale).astype(
        jnp.bfloat16
    )
    keys = project(whole, w_attn[1])
    values = project(whole, w_attn[2])
    every_prompt = lax.all_gather(prompts, "dp", axis=0, tiled=True)
    flat = every_prompt.reshape(-1, every_prompt.shape[2])
    prompt_key = project(flat, w_attn[1])
    prompt_value = project(flat, w_attn[2])
    prompt_len = prompts.shape[1]
    prompt_rows = prompt_key.shape[0]
    lens = lengths[0]
    texts_here = lens.shape[0]
    text_ids = jnp.arange(texts_here, dtype=jnp.int32)
    ends = jnp.sum(jnp.where(text_ids[None, :] <= text_ids[:, None], lens[None, :], 0), axis=1)
    position = jnp.arange(tok_dev, dtype=jnp.int32)
    seg = jnp.sum((position[:, None] >= ends[None, :]).astype(jnp.int32), axis=1)
    tok_group = jnp.sum(jnp.where(seg[:, None] == text_ids[None, :], groups[None, :], 0), axis=1)
    key_group = jnp.arange(prompt_rows, dtype=jnp.int32) // prompt_len
    all_keys = jnp.concatenate([keys, prompt_key], axis=0).reshape(-1, heads_here, HEAD_DIM)
    all_values = jnp.concatenate([values, prompt_value], axis=0).reshape(-1, heads_here, HEAD_DIM)
    block = min(512, tok_dev)

    def attend(number):
        start = number * block
        q_block = lax.dynamic_slice_in_dim(query, start, block, 0).reshape(
            block, heads_here, HEAD_DIM
        )
        seg_block = lax.dynamic_slice_in_dim(seg, start, block, 0)
        group_block = lax.dynamic_slice_in_dim(tok_group, start, block, 0)
        allowed = jnp.concatenate(
            [seg_block[:, None] == seg[None, :], group_block[:, None] == key_group[None, :]], axis=1
        )
        logits = jnp.einsum("qhe,khe->hqk", q_block, all_keys, preferred_element_type=jnp.float32)
        logits = jnp.where(allowed[None], logits, jnp.float32(-1e30))
        top = jnp.max(logits, axis=2, keepdims=True)
        weights = jnp.exp(logits - top)
        total = jnp.sum(weights, axis=2, keepdims=True)
        probs = (weights / total).astype(jnp.bfloat16)
        mixed = jnp.einsum("hqk,khe->qhe", probs, all_values, preferred_element_type=jnp.float32)
        return mixed.astype(jnp.bfloat16).reshape(block, columns)

    context = lax.map(attend, jnp.arange(tok_dev // block, dtype=jnp.int32)).reshape(
        tok_dev, columns
    )
    my_start = lax.axis_index("tensor") * shard_rows
    attn_part = lax.psum_scatter(
        jnp.dot(context, w_out, preferred_element_type=jnp.float32),
        "tensor",
        scatter_dimension=0,
        tiled=True,
    )
    normed_rows = layer_norm(
        tokens.astype(jnp.float32) + attn_part, norm_gain[0], norm_bias[0]
    ).astype(jnp.bfloat16)
    expanded = jax.nn.gelu(
        jnp.dot(
            lax.all_gather(normed_rows, "tensor", axis=0, tiled=True),
            w_in,
            preferred_element_type=jnp.float32,
        )
        + b_in,
        approximate=False,
    ).astype(jnp.bfloat16)
    reduced = lax.psum_scatter(
        jnp.dot(expanded, w_down, preferred_element_type=jnp.float32).astype(jnp.bfloat16),
        "tensor",
        scatter_dimension=0,
        tiled=True,
    ).astype(jnp.float32)
    output = layer_norm(
        normed_rows.astype(jnp.float32) + reduced, norm_gain[1], norm_bias[1]
    ).astype(jnp.bfloat16)
    seg_rows = lax.dynamic_slice_in_dim(seg, my_start, shard_rows, 0)
    member = (text_ids[:, None] == seg_rows[None, :]).astype(jnp.bfloat16)
    partial_sums = jnp.dot(member, output, preferred_element_type=jnp.float32)
    pooled_sums = lax.psum_scatter(partial_sums, "tensor", scatter_dimension=0, tiled=True)
    mine = pooled_sums.shape[0]
    my_lens = lax.dynamic_slice_in_dim(lens, lax.axis_index("tensor") * mine, mine, 0)
    pooled = pooled_sums / my_lens[:, None].astype(jnp.float32)
    square = jnp.mean(pooled * pooled, axis=1, keepdims=True)
    embedding = (pooled * lax.rsqrt(square + 1e-06)).astype(jnp.bfloat16)
    asked_vectors, asked_rows = (
        lax.all_gather(embedding, "dp", axis=0, tiled=True),
        lax.all_gather(candidates, "dp", axis=0, tiled=True),
    )
    held = index_rows.shape[0]
    local_rows = asked_rows - lax.axis_index("dp") * held
    owned = (local_rows >= 0) & (local_rows < held)
    table = jnp.dot(asked_vectors, index_rows.T, preferred_element_type=jnp.float32) * D ** (-0.5)
    picked = jnp.take_along_axis(table, jnp.clip(local_rows, 0, held - 1), axis=1)
    picked = jnp.where(owned, picked, jnp.float32(0.0))
    return lax.psum_scatter(
        picked.astype(jnp.bfloat16), "dp", scatter_dimension=0, tiled=True
    ).astype(jnp.float32)


def solution(mesh):
    placed = (
        P(("dp", "tensor"), None),
        P("dp", None, None),
        P(None, None, "tensor"),
        P("tensor", None),
        P(),
        P(),
        P(None, "tensor"),
        P("tensor"),
        P("tensor", None),
        P("dp", None),
        P("dp", None),
        P("dp"),
        P(("dp", "tensor"), None),
    )
    return jax.shard_map(
        shards, mesh=mesh, in_specs=placed, out_specs=P(("dp", "tensor"), None), check_vma=False
    )
```

```python
import functools

import jax
import jax.numpy as jnp
from jax import lax
from jax.experimental import pallas as pl
from jax.experimental.pallas import tpu as pltpu
from jax.sharding import PartitionSpec as P

D = 1024
HEAD_DIM = 64
KEY_TILE = 256
QUERY_TILE = 256
HEADS_STEP = 4


def layer_norm(values, gain, bias):
    mean = jnp.mean(values, axis=-1, keepdims=True)
    centred = values - mean
    var = jnp.mean(centred * centred, axis=-1, keepdims=True)
    return centred * lax.rsqrt(var + 1e-05) * gain + bias


def attention_kernel(
    bounds_ref, q_ref, k_ref, v_ref, qseg_ref, qgrp_ref, kseg_ref, kgrp_ref, out_ref, *, near
):
    tile = pl.program_id(0)
    first, last = bounds_ref[0, tile], bounds_ref[1, tile]
    q_seg, q_grp = qseg_ref[...], qgrp_ref[...]
    prompt_tiles = (k_ref.shape[1] - near) // KEY_TILE
    tn = (((0,), (0,)), ((), ()))

    def update(start, allowed, state):
        new = []
        for head in range(HEADS_STEP):
            top, total, acc = state[head]
            rows = pl.ds(head * HEAD_DIM, HEAD_DIM)
            logits = lax.dot_general(
                k_ref[rows, pl.ds(start, KEY_TILE)],
                q_ref[rows, :],
                tn,
                preferred_element_type=jnp.float32,
            )
            logits = jnp.where(allowed, logits, -1e30)
            peak = jnp.maximum(top, jnp.max(logits, axis=0, keepdims=True))
            weights = jnp.exp(logits - peak)
            fade = jnp.exp(top - peak)
            total = total * fade + jnp.sum(weights, axis=0, keepdims=True)
            mixed = jnp.dot(
                v_ref[rows, pl.ds(start, KEY_TILE)],
                weights.astype(jnp.bfloat16),
                preferred_element_type=jnp.float32,
            )
            new.append((peak, total, acc * fade + mixed))
        return tuple(new)

    def near_step(number, state):
        start = pl.multiple_of(number * KEY_TILE, KEY_TILE)
        return update(start, kseg_ref[pl.ds(start, KEY_TILE), :] == q_seg, state)

    def prompt_step(number, state):
        start = pl.multiple_of(number * KEY_TILE, KEY_TILE)
        allowed = kgrp_ref[pl.ds(start, KEY_TILE), :] == q_grp
        return update(pl.multiple_of(near + start, KEY_TILE), allowed, state)

    row = (1, QUERY_TILE)
    state = tuple(
        (
            jnp.full(row, -1e30, jnp.float32),
            jnp.zeros(row, jnp.float32),
            jnp.zeros((HEAD_DIM, QUERY_TILE), jnp.float32),
        )
        for _ in range(HEADS_STEP)
    )
    state = lax.fori_loop(first, last, near_step, state)
    state = lax.fori_loop(0, prompt_tiles, prompt_step, state)
    for head in range(HEADS_STEP):
        _, total, acc = state[head]
        out_ref[pl.ds(head * HEAD_DIM, HEAD_DIM), :] = (acc / total).astype(jnp.bfloat16)


def attention(bounds, query, keys, values, q_seg, q_grp, k_seg, k_grp):
    width, rows = query.shape
    every = keys.shape[1]
    near = k_seg.shape[0]
    step = HEADS_STEP * HEAD_DIM
    by_tile = pl.BlockSpec((1, QUERY_TILE), lambda i, j, b: (0, i))
    return pl.pallas_call(
        functools.partial(attention_kernel, near=near),
        out_shape=jax.ShapeDtypeStruct((width, rows), jnp.bfloat16),
        grid_spec=pltpu.PrefetchScalarGridSpec(
            num_scalar_prefetch=1,
            grid=(rows // QUERY_TILE, width // step),
            in_specs=[
                pl.BlockSpec((step, QUERY_TILE), lambda i, j, b: (j, i)),
                pl.BlockSpec((step, every), lambda i, j, b: (j, 0)),
                pl.BlockSpec((step, every), lambda i, j, b: (j, 0)),
                by_tile,
                by_tile,
                pl.BlockSpec((near, 1), lambda i, j, b: (0, 0)),
                pl.BlockSpec((every - near, 1), lambda i, j, b: (0, 0)),
            ],
            out_specs=pl.BlockSpec((step, QUERY_TILE), lambda i, j, b: (j, i)),
        ),
        compiler_params=pltpu.CompilerParams(vmem_limit_bytes=40 << 20),
        cost_estimate=pl.CostEstimate(
            flops=4 * width * rows * 1280, bytes_accessed=8 << 20, transcendentals=16 * rows * 1280
        ),
    )(bounds, query, keys, values, q_seg, q_grp, k_seg, k_grp)


def pick(table, asked):
    texts, held = table.shape
    place = jnp.arange(held, dtype=jnp.int32)
    return jnp.sum(
        jnp.where(asked[:, :, None] == place[None, None, :], table[:, None, :], 0.0), axis=2
    )


def shards(
    tokens,
    prompts,
    w_attn,
    w_out,
    norm_gain,
    norm_bias,
    w_in,
    b_in,
    w_down,
    index_rows,
    lengths,
    groups,
    candidates,
):
    shard_rows = tokens.shape[0]
    parts = lax.axis_size("tensor")
    copies = lax.axis_size("dp")
    me = lax.axis_index("tensor")
    columns = w_attn.shape[2]
    scale = HEAD_DIM ** (-0.5)

    def own_part(weight):
        rows = weight.shape[0] // copies
        return lax.dynamic_slice_in_dim(weight, lax.axis_index("dp") * rows, rows, 0)

    def gather_parts(pieces, width):
        flat = [piece.reshape(-1, width) for piece in pieces]
        got = lax.all_gather(
            jnp.concatenate(flat, axis=0), ("tensor", "dp"), axis=0, tiled=False
        )
        back, at = [], 0
        for piece in flat:
            back.append(got[:, at : at + piece.shape[0]])
            at += piece.shape[0]
        return back

    before = lax.ppermute(tokens, "tensor", [(i, i + 1) for i in range(parts - 1)])
    after = lax.ppermute(tokens, "tensor", [(i + 1, i) for i in range(parts - 1)])
    my_prompts = prompts.reshape(-1, D)
    prompt_rows = my_prompts.shape[0] // parts
    prompt_part = lax.dynamic_slice_in_dim(my_prompts, me * prompt_rows, prompt_rows, 0)
    early = gather_parts(
        [own_part(w_attn.reshape(-1, columns)), own_part(w_out), prompt_part], columns
    )
    attn_all = early[0].reshape(parts, 3, D, columns)
    out_all = early[1].reshape(-1, D)
    flat_prompts = early[2].reshape(parts, copies, -1, D).swapaxes(0, 1).reshape(-1, D)
    late = gather_parts([own_part(w_in), own_part(w_down)], D)
    in_all = late[0].reshape(parts, D, -1)
    down_all = late[1].reshape(-1, D)
    b_all = lax.all_gather(b_in, "tensor", axis=0, tiled=True)

    lens = lengths[0]
    texts_here = lens.shape[0]
    text_ids = jnp.arange(texts_here, dtype=jnp.int32)
    ends = jnp.sum(jnp.where(text_ids[None, :] <= text_ids[:, None], lens[None, :], 0), axis=1)
    near = 3 * shard_rows
    place = jnp.arange(near, dtype=jnp.int32) + (me - 1) * shard_rows
    seg = jnp.sum((place[:, None] >= ends[None, :]).astype(jnp.int32), axis=1)
    k_seg = jnp.where(place >= 0, seg, -1)
    q_seg = seg[shard_rows : 2 * shard_rows]
    q_grp = jnp.sum(jnp.where(q_seg[:, None] == text_ids[None, :], groups[None, :], 0), axis=1)
    k_grp = jnp.arange(flat_prompts.shape[0], dtype=jnp.int32) // prompts.shape[1]
    by_tile = q_seg.reshape(-1, QUERY_TILE)
    least, most = by_tile[:, :1], by_tile[:, -1:]
    first = jnp.sum((k_seg[None, :] < least).astype(jnp.int32), axis=1) // KEY_TILE
    inside = jnp.sum((k_seg[None, :] <= most).astype(jnp.int32), axis=1)
    last = (inside + KEY_TILE - 1) // KEY_TILE
    bounds = jnp.stack([first, last])

    rows = jnp.concatenate([before, tokens, after, flat_prompts], axis=0)

    def project(weight, block):
        return jnp.einsum("tdc,nd->tcn", weight, block, preferred_element_type=jnp.float32)

    query = (project(attn_all[:, 0], tokens) * scale).astype(jnp.bfloat16).reshape(D, -1)
    keys = project(attn_all[:, 1], rows).astype(jnp.bfloat16).reshape(D, -1)
    values = project(attn_all[:, 2], rows).astype(jnp.bfloat16).reshape(D, -1)
    context = attention(
        bounds, query, keys, values, q_seg[None], q_grp[None], k_seg[:, None], k_grp[:, None]
    )
    attended = jnp.einsum("cn,cd->nd", context, out_all, preferred_element_type=jnp.float32)
    normed = layer_norm(
        tokens.astype(jnp.float32) + attended, norm_gain[0], norm_bias[0]
    ).astype(jnp.bfloat16)
    reduced = jnp.zeros((shard_rows, D), jnp.float32)
    units = b_in.shape[0]
    for part in range(parts):
        cols = slice(part * units, (part + 1) * units)
        expanded = jax.nn.gelu(
            jnp.dot(normed, in_all[part], preferred_element_type=jnp.float32) + b_all[cols],
            approximate=False,
        ).astype(jnp.bfloat16)
        reduced += jnp.dot(expanded, down_all[cols], preferred_element_type=jnp.float32)
    output = layer_norm(
        normed.astype(jnp.float32) + reduced, norm_gain[1], norm_bias[1]
    ).astype(jnp.bfloat16)
    member = (text_ids[:, None] == q_seg[None, :]).astype(jnp.bfloat16)
    partial_sums = jnp.dot(member, output, preferred_element_type=jnp.float32)
    pooled_sums = jnp.sum(
        lax.all_to_all(
            partial_sums.reshape(parts, -1, D), "tensor", split_axis=0, concat_axis=0
        ),
        axis=0,
    )
    mine = pooled_sums.shape[0]
    my_lens = lax.dynamic_slice_in_dim(lens, me * mine, mine, 0)
    pooled = pooled_sums / my_lens[:, None].astype(jnp.float32)
    square = jnp.mean(pooled * pooled, axis=1, keepdims=True)
    embedding = (pooled * lax.rsqrt(square + 1e-06)).astype(jnp.bfloat16)
    asked_vectors, asked_rows = (
        lax.all_gather(embedding, "dp", axis=0, tiled=True),
        lax.all_gather(candidates, "dp", axis=0, tiled=True),
    )
    held = index_rows.shape[0]
    local_rows = asked_rows - lax.axis_index("dp") * held
    table = jnp.dot(asked_vectors, index_rows.T, preferred_element_type=jnp.float32) * D ** (-0.5)
    picked = pick(table, local_rows)
    answers = lax.all_to_all(
        picked.astype(jnp.bfloat16).reshape(copies, -1, picked.shape[1]),
        "dp",
        split_axis=0,
        concat_axis=0,
    )
    return jnp.sum(answers.astype(jnp.float32), axis=0)


def solution(mesh):
    placed = (
        P(("dp", "tensor"), None),
        P("dp", None, None),
        P(None, None, "tensor"),
        P("tensor", None),
        P(),
        P(),
        P(None, "tensor"),
        P("tensor"),
        P("tensor", None),
        P("dp", None),
        P("dp", None),
        P("dp"),
        P(("dp", "tensor"), None),
    )
    return jax.shard_map(
        shards, mesh=mesh, in_specs=placed, out_specs=P(("dp", "tensor"), None), check_vma=False
    )
```
